512 devices in a mesh: space: 64 (over z_lo, y, core), snap: 8 (over z_hi, x).
Axes of the slice: x: 4, y: 4, z: 16 (z_hi: 2, z_lo: 8; z = z_hi * 8 + z_lo), core: 2. Of those that a mesh axis runs over, the one named last changes fastest.
Arguments:
- snapshots: float32 [32768, 2048], P('space', 'snap'), may hold values from -6 to 6
- following: float32 [32768], P('space'), may hold values from -6 to 6
- mass: float32 [32768], P('space'), may hold values from 9.155274e-06 to 9.1552734e-05
Outputs:
- gram: float32 [2048, 2048], P('space', 'snap')
- lagged_gram: float32 [2048, 2048], P('space', 'snap')
The draws below stay inside these ranges and needn't reach their ends.
All inputs are finite; a program needn't handle non-finite values.
Results may differ from the reference program's by a relative error of at most 0.00005.
Values sent between devices are 32-bit elements; how exact they have to be, the bound alone decides.
No kernel may reach another device: no remote copies, remote signals or barrier semaphores. Data moves between devices by JAX's collectives and lax.ppermute only.
A program may use at most 64 MiB of HBM per device.

```python
import math
import jax
import jax.numpy as jnp
from jax import lax

NPTS = 32768
M = 2048


def level_of(rng, shape, cuts, smallest, top_value):
    def one(dim, blocks):
        heights = jax.random.uniform(jax.random.fold_in(jax.random.fold_in(rng, 6), dim), (blocks,), jnp.float32, smallest / len(cuts), top_value / len(cuts))
        return jnp.repeat(jnp.exp(heights), shape[dim] // blocks).reshape((-1,) + (1,) * (len(shape) - dim - 1))

    factor_of = one(*cuts[0])
    for cut in cuts[1:]:
        factor_of = factor_of * one(*cut)
    return factor_of


def scatter_about(key, shape, width, reach, shards=(), kind=jnp.bfloat16):
    gain = level_of(key, shape, shards, -0.22, 0.18) if shards else 1.0
    result = jax.random.normal(key, shape, jnp.float32) * width * gain
    return jnp.minimum(jnp.maximum(result, -reach), reach).astype(kind)


def setup_inputs(seed: int = 0) -> dict:
    arg_keys = jax.random.split(jax.random.key(seed), 4)
    snapshots = scatter_about(arg_keys[0], (NPTS, M), 1.0, 6.0, ((0, 64), (1, 8)), jnp.float32)
    following = scatter_about(arg_keys[1], (NPTS,), 1.0, 6.0, ((0, 64),), jnp.float32)
    mass = jnp.clip(jnp.exp(math.log(9.1552734375e-05) - 2.3025851 * jax.random.uniform(arg_keys[2], (NPTS,), jnp.float32) ** level_of(arg_keys[2], (NPTS,), ((0, 64),), -0.2, 0.2)), 9.15527380129788e-06, 9.1552734375e-05)
    return dict(snapshots=snapshots, following=following, mass=mass)


def reference(snapshots, following, mass):
    weighted = mass[:, None] * snapshots
    successors = jnp.concatenate([snapshots[:, 1:], following[:, None]], axis=1)
    dims = (((0,), (0,)), ((), ()))
    gram = lax.dot_general(weighted, snapshots, dims, precision=lax.Precision.HIGHEST, preferred_element_type=jnp.float32)
    lagged_gram = lax.dot_general(weighted, successors, dims, precision=lax.Precision.HIGHEST, preferred_element_type=jnp.float32)
    return gram, lagged_gram
```

```python
import jax
import jax.numpy as jnp
import numpy as np
from jax import lax
from jax.sharding import Mesh, PartitionSpec as P

NAMES = ("zl", "y", "c", "zh", "x")
SIZES = (8, 4, 2, 2, 4)
ZL, Y, C, ZH, X = SIZES
FLAT = ZL * Y * C * ZH * X


def routes(move):
    pairs = []
    for source in range(FLAT):
        zl, y, c, zh, x = (int(v) for v in np.unravel_index(source, SIZES))
        target = move(zh * ZL + zl, y, c, x)
        if target is None:
            continue
        z, y, c, x = target
        z = z % (ZH * ZL)
        place = (z % ZL, y % Y, c % C, z // ZL, x % X)
        pairs.append((source, int(np.ravel_multi_index(place, SIZES))))
    return pairs


def send(value, move):
    return lax.ppermute(value, NAMES, routes(move))


def columns_on(step):
    def move(z, y, c, x):
        block = (z // ZL * X + x - step) % (ZH * X)
        return (block // X * ZL + z % ZL, y, c, block % X)

    return move


def across(z, y, c, x):
    return (z + ZL, y, c, x)


def home(z, y, c, x):
    half = ZL // 2
    if half <= z < ZL:
        return (z + half, y, c, x)
    if ZL <= z < ZL + half:
        return (z - half, y, c, x)
    return None


def product(rows, columns):
    return lax.dot_general(
        rows,
        columns,
        (((0,), (0,)), ((), ())),
        precision=lax.Precision.HIGH,
        preferred_element_type=jnp.float32,
    )


def shards(snapshots, following, mass):
    points, width = snapshots.shape
    r = width // (Y * C)
    x, zh, zl = lax.axis_index("x"), lax.axis_index("zh"), lax.axis_index("zl")
    block = zh * X + x

    partner = send(snapshots, across)
    blocks = [snapshots] + [
        send(snapshots, lambda z, y, c, x, k=k: (z, y, c, x - k)) for k in (1, 3, 2)
    ]
    blocks = [blocks[0], blocks[1], blocks[3], blocks[2]]
    first = snapshots[:, 0]
    after_own = send(first, columns_on(1))
    after_partner = send(first, columns_on(X + 1))
    after_own = jnp.where(block == ZH * X - 1, following, after_own)
    after_partner = jnp.where(block == X - 1, following, after_partner)

    after = jnp.stack([after_own, after_partner], axis=1) * mass[:, None]
    edge = jnp.stack([product(after, b) for b in blocks])
    edge = edge.reshape(X, 2, Y * C, r).transpose(2, 1, 0, 3)
    edge = edge.reshape(Y * C, 1, 2 * X * r)

    def gram(columns):
        return jnp.concatenate(
            [product(b, columns).reshape(1, Y * C, r, width) for b in blocks]
        ).transpose(1, 0, 2, 3).reshape(Y * C, X * r, width)

    def scatter(value):
        moved = lax.all_to_all(value, ("y", "c"), 0, 0, tiled=True)
        return jnp.sum(moved, axis=0)

    own = gram(snapshots * mass[:, None])
    pad = jnp.zeros((Y * C, 7, width), jnp.float32)
    own = scatter(jnp.concatenate([own, edge, pad], axis=1))
    edge = own[X * r].reshape(2, X, r)
    own = own[: X * r].reshape(X, r, width)
    cross = scatter(gram(partner * mass[:, None])).reshape(X, r, width)

    edge = jnp.pad(edge.reshape(2 * X, 1, r), ((0, 0), (0, 7), (0, width - r)))
    both = jnp.concatenate([jnp.concatenate([own, cross]), edge], axis=1)
    slots = [
        lax.dynamic_index_in_dim(
            both, ((s // X + zh) % 2) * X + (s - x + X) % X, 0, keepdims=True
        )
        for s in range(ZL)
    ]
    moved = lax.all_to_all(jnp.concatenate(slots), "zl", 0, 0, tiled=True)
    tile = jnp.sum(moved, axis=0)
    other = send(tile, home)
    tile = jnp.where((zl >= X) == (zh == 0), other, tile)
    tile_gram = tile[:r]
    last = tile[r, :r]
    return tile_gram, jnp.concatenate([tile_gram[:, 1:], last[:, None]], axis=1)


def solution(mesh):
    fine = Mesh(mesh.devices.reshape(SIZES), NAMES)
    rows, columns = ("zl", "y", "c"), ("zh", "x")
    return jax.shard_map(
        shards,
        mesh=fine,
        in_specs=(P(rows, columns), P(rows), P(rows)),
        out_specs=(P(rows, columns), P(rows, columns)),
        check_vma=False,
    )
```

```python
import jax
import jax.numpy as jnp
import numpy as np
from jax import lax
from jax.sharding import Mesh, PartitionSpec as P

NAMES = ("zl", "y", "c", "zh", "x")
SIZES = (8, 4, 2, 2, 4)
ZL, Y, C, ZH, X = SIZES
FLAT = ZL * Y * C * ZH * X


def routes(move):
    pairs = []
    for source in range(FLAT):
        zl, y, c, zh, x = (int(v) for v in np.unravel_index(source, SIZES))
        target = move(zh * ZL + zl, y, c, x)
        if target is None:
            continue
        z, y, c, x = target
        z = z % (ZH * ZL)
        place = (z % ZL, y % Y, c % C, z // ZL, x % X)
        pairs.append((source, int(np.ravel_multi_index(place, SIZES))))
    return pairs


def send(value, move):
    return lax.ppermute(value, NAMES, routes(move))


def columns_on(step):
    def move(z, y, c, x):
        block = (z // ZL * X + x - step) % (ZH * X)
        return (block // X * ZL + z % ZL, y, c, block % X)

    return move


def across(z, y, c, x):
    return (z + ZL, y, c, x)


def home(z, y, c, x):
    half = ZL // 2
    if half <= z < ZL:
        return (z + half, y, c, x)
    if ZL <= z < ZL + half:
        return (z - half, y, c, x)
    return None


def product(rows, columns):
    return lax.dot_general(
        rows,
        columns,
        (((0,), (0,)), ((), ())),
        precision=lax.Precision.HIGH,
        preferred_element_type=jnp.float32,
    )


def shards(snapshots, following, mass):
    points, width = snapshots.shape
    r = width // (Y * C)
    x, zh, zl = lax.axis_index("x"), lax.axis_index("zh"), lax.axis_index("zl")
    block = zh * X + x

    partner = send(snapshots, across)
    blocks = [snapshots] + [
        send(snapshots, lambda z, y, c, x, k=k: (z, y, c, x - k)) for k in (1, 3, 2)
    ]
    blocks = [blocks[0], blocks[1], blocks[3], blocks[2]]
    first, _ = lax.optimization_barrier((snapshots[:, 0], blocks[1]))
    after_own = send(first, columns_on(1))
    after_partner = send(first, columns_on(X + 1))
    after_own = jnp.where(block == ZH * X - 1, following, after_own)
    after_partner = jnp.where(block == X - 1, following, after_partner)

    after = jnp.stack([after_own, after_partner], axis=1) * mass[:, None]
    edge = jnp.stack([product(after, b) for b in blocks])
    edge = edge.reshape(X, 2, Y * C, r).transpose(2, 1, 0, 3)
    edge = edge.reshape(Y * C, 1, 2 * X * r)

    def gram(columns):
        return jnp.concatenate(
            [product(b, columns).reshape(1, Y * C, r, width) for b in blocks]
        ).transpose(1, 0, 2, 3).reshape(Y * C, X * r, width)

    def scatter(value):
        moved = lax.all_to_all(value, ("y", "c"), 0, 0, tiled=True)
        return jnp.sum(moved, axis=0)

    own = scatter(gram(snapshots * mass[:, None])).reshape(X, r, width)
    pad = jnp.zeros((Y * C, 7, width), jnp.float32)
    own, partner = lax.optimization_barrier((own, partner))
    cross = gram(partner * mass[:, None])
    cross = scatter(jnp.concatenate([cross, edge, pad], axis=1))
    edge = cross[X * r].reshape(2, X, r)
    cross = cross[: X * r].reshape(X, r, width)

    edge = jnp.pad(edge.reshape(2 * X, 1, r), ((0, 0), (0, 7), (0, width - r)))
    both = jnp.concatenate([jnp.concatenate([own, cross]), edge], axis=1)
    slots = [
        lax.dynamic_index_in_dim(
            both, ((s // X + zh) % 2) * X + (s - x + X) % X, 0, keepdims=True
        )
        for s in range(ZL)
    ]
    moved = lax.all_to_all(jnp.concatenate(slots), "zl", 0, 0, tiled=True)
    tile = jnp.sum(moved, axis=0)
    other = send(tile, home)
    tile = jnp.where((zl >= X) == (zh == 0), other, tile)
    tile_gram = tile[:r]
    last = tile[r, :r]
    return tile_gram, jnp.concatenate([tile_gram[:, 1:], last[:, None]], axis=1)


def solution(mesh):
    fine = Mesh(mesh.devices.reshape(SIZES), NAMES)
    rows, columns = ("zl", "y", "c"), ("zh", "x")
    return jax.shard_map(
        shards,
        mesh=fine,
        in_specs=(P(rows, columns), P(rows), P(rows)),
        out_specs=(P(rows, columns), P(rows, columns)),
        check_vma=False,
    )
```

```python
import jax
import jax.numpy as jnp
import numpy as np
from jax import lax
from jax.experimental import pallas as pl
from jax.experimental.pallas import tpu as pltpu
from jax.sharding import Mesh, PartitionSpec as P

NAMES = ("zl", "y", "c", "zh", "x")
SIZES = (8, 4, 2, 2, 4)
ZL, Y, C, ZH, X = SIZES
FLAT = ZL * Y * C * ZH * X
PAD = 8


def routes(move):
    pairs = []
    for source in range(FLAT):
        zl, y, c, zh, x = (int(v) for v in np.unravel_index(source, SIZES))
        target = move(zh * ZL + zl, y, c, x)
        if target is None:
            continue
        z, y, c, x = target
        z = z % (ZH * ZL)
        place = (z % ZL, y % Y, c % C, z // ZL, x % X)
        pairs.append((source, int(np.ravel_multi_index(place, SIZES))))
    return pairs


def send(value, move):
    return lax.ppermute(value, NAMES, routes(move))


def home(z, y, c, x):
    half = ZL // 2
    if half <= z < ZL:
        return (z + half, y, c, x)
    if ZL <= z < ZL + half:
        return (z - half, y, c, x)
    return None


def call(kernel, out, flops, *operands):
    return pl.pallas_call(
        kernel,
        out_shape=jax.ShapeDtypeStruct(out, jnp.float32),
        in_specs=[pl.BlockSpec(memory_space=pltpu.VMEM)] * len(operands),
        out_specs=pl.BlockSpec(memory_space=pltpu.VMEM),
        compiler_params=pltpu.CompilerParams(vmem_limit_bytes=48 << 20),
        cost_estimate=pl.CostEstimate(
            flops=flops, bytes_accessed=1 << 23, transcendentals=0
        ),
    )(*operands)


def split(value):
    high = value.astype(jnp.bfloat16)
    return high, (value - high.astype(jnp.float32)).astype(jnp.bfloat16)


def prepare(columns):
    high, low = split(columns.T)
    return high, jnp.concatenate([high, low], axis=0)


def product(prepared, rows):
    high, both = prepared
    size = high.shape[0]
    rows_high, rows_low = split(rows)
    part = jnp.dot(both, rows_high, preferred_element_type=jnp.float32)
    rest = jnp.dot(high, rows_low, preferred_element_type=jnp.float32)
    return part[:size] + part[size:] + rest


def scale_kernel(value_ref, weight_ref, out_ref):
    out_ref[...] = value_ref[...] * weight_ref[...]


def stack_kernel(*refs):
    for k, ref in enumerate(refs[:-1]):
        refs[-1][k] = ref[...]


def first_kernel(columns_ref, *refs):
    out_ref = refs[-1]
    width = columns_ref.shape[1]
    r = width // (Y * C)
    prepared = prepare(columns_ref[...])
    for k, ref in enumerate(refs[:-1]):
        value = product(prepared, ref[...]).T
        out_ref[:, k * r : (k + 1) * r, :] = value.reshape(Y * C, r, width)


def rows_of(values, g):
    r = values[0].shape[1] // (Y * C)
    return jnp.concatenate([value[:, g * r : (g + 1) * r] for value in values], axis=1)


def edge_kernel(after_ref, *refs):
    high, low = split(after_ref[...])
    after = (high, jnp.concatenate([high, low], axis=0))
    values = [product(after, ref[...]) for ref in refs[:-1]]
    for g in range(Y * C):
        refs[-1][g] = rows_of(values, g)


def second_kernel(
    far_ref, edges_ref, same_ref, other_ref, blocks_ref, others_ref, out_ref
):
    count, points, width = blocks_ref.shape
    size = other_ref.shape[1]
    r = width // (Y * C)
    here = prepare(same_ref[:points])
    there = prepare(other_ref[...])
    edge_high, edge_low = split(far_ref[...])
    edge = (edge_high, jnp.concatenate([edge_high, edge_low], axis=0))
    edges = []
    for k in range(count):
        value = product(here, blocks_ref[k]) + product(there, others_ref[k])
        out_ref[:, k * r : (k + 1) * r, :] = value.T.reshape(Y * C, r, size)
        edges.append(product(edge, blocks_ref[k]))
    for g in range(Y * C):
        out_ref[g, count * r :, :] = edges_ref[g] + rows_of(edges, g)


def shards(snapshots, following, mass):
    points, width = snapshots.shape
    half, r = width // 2, width // (Y * C)
    x, zh, zl = lax.axis_index("x"), lax.axis_index("zh"), lax.axis_index("zl")
    core = lax.axis_index("c")

    def along_x(value, k):
        return send(value, lambda z, y, c, x: (z, y, c, x - k))

    def facing(value, k):
        return send(value, lambda z, y, c, x: (z + ZL, y, c ^ k, x))

    def turned(value):
        return lax.dynamic_slice_in_dim(
            jnp.concatenate([value, value]), (X - x) & (X - 1), X, 0
        )

    def sides(own, cross):
        return jnp.where(
            zh == 0,
            jnp.concatenate([own, cross]),
            jnp.concatenate([cross, own]),
        )

    columns = snapshots * mass[:, None]
    same, other = (
        lax.dynamic_slice_in_dim(columns, half * (core ^ k), half, 1) for k in (0, 1)
    )
    other = facing(other, 1)
    blocks = [snapshots, along_x(snapshots, 1)]
    behind = along_x(snapshots, X - 1)
    again, late, same, _ = lax.optimization_barrier((snapshots, mass, same, blocks[1]))
    next_first = blocks[1][:, 0] * mass
    folded = jnp.pad(next_first.reshape(-1, half), ((0, PAD - points // half), (0, 0)))
    same = facing(jnp.concatenate([same, folded], axis=0), 0)
    blocks += [along_x(again, 2), behind]
    weighted = call(scale_kernel, (points, width), 1 << 38, again, late[:, None])

    own = call(
        first_kernel, (Y * C, X * r, width), 1 << 30, weighted, *blocks
    )
    own = lax.all_to_all(own, ("y", "c"), 0, 0, tiled=True)
    own = turned(jnp.sum(own, axis=0).reshape(X, r, width))
    stack = call(stack_kernel, (X, points, width), 1 << 38, *blocks)
    others = send(stack, lambda z, y, c, x: (z, y, c ^ 1, x))
    after = jnp.pad(jnp.stack([next_first, following * mass]), ((0, PAD - 2), (0, 0)))
    edges = call(edge_kernel, (Y * C, PAD, X * r), 1 << 38, after, *blocks)
    own, stack, others, same, other, edges = lax.optimization_barrier(
        (own, stack, others, same, other, edges)
    )

    far = same[points : points + points // half].reshape(1, points)
    far = jnp.pad(far, ((2, PAD - 3), (0, 0)))
    cross = call(
        second_kernel,
        (Y * C, X * r + PAD, half),
        1 << 30,
        far,
        edges,
        same,
        other,
        stack,
        others,
    )
    cross = lax.all_to_all(cross, ("y", "c"), 0, 0, tiled=True)
    cross = jnp.sum(cross.reshape(Y, C, X * r + PAD, half), axis=0)
    near, end, far = jnp.sum(cross[:, X * r : X * r + 3], axis=0)
    inner = x < X - 1
    edges = jnp.stack(
        [
            jnp.where(inner, near, jnp.where(zh == 0, far, end)),
            jnp.where(inner, far, jnp.where(zh == 0, end, near)),
        ]
    ).reshape(2, X, 1, r)
    edges = jnp.pad(edges, ((0, 0), (0, 0), (0, PAD - 1), (0, width - r)))
    cross = jnp.concatenate([cross[0, : X * r], cross[1, : X * r]], axis=1)
    cross = turned(jnp.concatenate([cross.reshape(X, r, width), edges[1]], axis=1))
    own = jnp.concatenate([own, turned(edges[0])], axis=1)
    total = lax.all_to_all(sides(own, cross), "zl", 0, 0, tiled=True)
    total = jnp.sum(total, axis=0)
    moved = (zl >= X) == (zh == 0)
    total = jnp.where(moved, send(total, home), total)
    tile = total[:r]
    return tile, jnp.concatenate([tile[:, 1:], total[r, :r, None]], axis=1)


def solution(mesh):
    fine = Mesh(mesh.devices.reshape(SIZES), NAMES)
    rows, columns = ("zl", "y", "c"), ("zh", "x")
    return jax.shard_map(
        shards,
        mesh=fine,
        in_specs=(P(rows, columns), P(rows), P(rows)),
        out_specs=(P(rows, columns), P(rows, columns)),
        check_vma=False,
    )
```

```python
import jax
import jax.numpy as jnp
import numpy as np
from jax import lax
from jax.experimental import pallas as pl
from jax.experimental.pallas import tpu as pltpu
from jax.sharding import Mesh, PartitionSpec as P

NAMES = ("zl", "y", "c", "zh", "x")
SIZES = (8, 4, 2, 2, 4)
ZL, Y, C, ZH, X = SIZES
FLAT = ZL * Y * C * ZH * X
PAD = 8


def routes(move):
    pairs = []
    for source in range(FLAT):
        zl, y, c, zh, x = (int(v) for v in np.unravel_index(source, SIZES))
        target = move(zh * ZL + zl, y, c, x)
        if target is None:
            continue
        z, y, c, x = target
        z = z % (ZH * ZL)
        place = (z % ZL, y % Y, c % C, z // ZL, x % X)
        pairs.append((source, int(np.ravel_multi_index(place, SIZES))))
    return pairs


def send(value, move):
    return lax.ppermute(value, NAMES, routes(move))


def home(z, y, c, x):
    half = ZL // 2
    if half <= z < ZL:
        return (z + half, y, c, x)
    if ZL <= z < ZL + half:
        return (z - half, y, c, x)
    return None


def call(kernel, out, flops, *operands):
    return pl.pallas_call(
        kernel,
        out_shape=jax.ShapeDtypeStruct(out, jnp.float32),
        in_specs=[pl.BlockSpec(memory_space=pltpu.VMEM)] * len(operands),
        out_specs=pl.BlockSpec(memory_space=pltpu.VMEM),
        compiler_params=pltpu.CompilerParams(vmem_limit_bytes=20 << 20),
        cost_estimate=pl.CostEstimate(
            flops=flops, bytes_accessed=1 << 23, transcendentals=0
        ),
    )(*operands)


def split(value):
    high = value.astype(jnp.bfloat16)
    return high, (value - high.astype(jnp.float32)).astype(jnp.bfloat16)


def prepare(columns):
    high, low = split(columns.T)
    return high, jnp.concatenate([high, low], axis=0)


def product(prepared, rows):
    high, both = prepared
    size = high.shape[0]
    rows_high, rows_low = split(rows)
    part = jnp.dot(both, rows_high, preferred_element_type=jnp.float32)
    rest = jnp.dot(high, rows_low, preferred_element_type=jnp.float32)
    return part[:size] + part[size:] + rest


def scale_kernel(value_ref, weight_ref, out_ref):
    out_ref[...] = value_ref[...] * weight_ref[...]


def stack_kernel(*refs):
    for k, ref in enumerate(refs[:-1]):
        refs[-1][k] = ref[...]


def first_kernel(columns_ref, *refs):
    out_ref = refs[-1]
    width = columns_ref.shape[1]
    r = width // (Y * C)
    prepared = prepare(columns_ref[...])
    for k, ref in enumerate(refs[:-1]):
        value = product(prepared, ref[...]).T
        out_ref[:, k * r : (k + 1) * r, :] = value.reshape(Y * C, r, width)


def rows_of(values, g):
    r = values[0].shape[1] // (Y * C)
    return jnp.concatenate([value[:, g * r : (g + 1) * r] for value in values], axis=1)


def edge_kernel(after_ref, *refs):
    high, low = split(after_ref[...])
    after = (high, jnp.concatenate([high, low], axis=0))
    values = [product(after, ref[...]) for ref in refs[:-1]]
    for g in range(Y * C):
        refs[-1][g] = rows_of(values, g)


def second_kernel(
    far_ref, edges_ref, same_ref, other_ref, blocks_ref, others_ref, out_ref
):
    count, points, width = blocks_ref.shape
    size = other_ref.shape[1]
    r = width // (Y * C)
    here = prepare(same_ref[:points])
    there = prepare(other_ref[...])
    edge_high, edge_low = split(far_ref[...])
    edge = (edge_high, jnp.concatenate([edge_high, edge_low], axis=0))
    edges = []
    for k in range(count):
        value = product(here, blocks_ref[k]) + product(there, others_ref[k])
        out_ref[:, k * r : (k + 1) * r, :] = value.T.reshape(Y * C, r, size)
        edges.append(product(edge, blocks_ref[k]))
    for g in range(Y * C):
        out_ref[g, count * r :, :] = edges_ref[g] + rows_of(edges, g)


def finish_kernel(moved_ref, mine_ref, sent_ref, tile_ref, later_ref):
    r, width = tile_ref.shape
    half = width // 2
    value = jnp.where(moved_ref[0] > 0, sent_ref[...], mine_ref[...])
    tile = jnp.concatenate([value[:r], value[r : 2 * r]], axis=1)
    row = lax.broadcasted_iota(jnp.int32, (r, half), 0)
    lane = lax.broadcasted_iota(jnp.int32, (r, half), 1)
    edge = jnp.broadcast_to(value[2 * r : 2 * r + 1], (r, half))
    edge = jnp.sum(jnp.where(row == lane, edge, 0.0), axis=1, keepdims=True)
    lane = lax.broadcasted_iota(jnp.int32, (r, width), 1)
    tile_ref[...] = tile
    later_ref[...] = jnp.where(
        lane == width - 1, edge, pltpu.roll(tile, width - 1, axis=1)
    )


def finish(moved, mine, sent):
    r, width = (mine.shape[0] - PAD) // 2, 2 * mine.shape[1]
    vmem = pl.BlockSpec(memory_space=pltpu.VMEM)
    return pl.pallas_call(
        finish_kernel,
        out_shape=[jax.ShapeDtypeStruct((r, width), jnp.float32)] * 2,
        in_specs=[pl.BlockSpec(memory_space=pltpu.SMEM), vmem, vmem],
        out_specs=[vmem, vmem],
    )(moved.astype(jnp.int32).reshape(1), mine, sent)


def shards(snapshots, following, mass):
    points, width = snapshots.shape
    half, r = width // 2, width // (Y * C)
    x, zh, zl = lax.axis_index("x"), lax.axis_index("zh"), lax.axis_index("zl")
    core = lax.axis_index("c")

    def along_x(value, k):
        return send(value, lambda z, y, c, x: (z, y, c, x - k))

    def facing(value, k):
        return send(value, lambda z, y, c, x: (z + ZL, y, c ^ k, x))

    def turned(value):
        return lax.dynamic_slice_in_dim(
            jnp.concatenate([value, value]), (X - x) & (X - 1), X, 0
        )

    def sides(own, cross):
        return jnp.where(
            zh == 0,
            jnp.concatenate([own, cross]),
            jnp.concatenate([cross, own]),
        )

    columns = snapshots * mass[:, None]
    same, other = (
        lax.dynamic_slice_in_dim(columns, half * (core ^ k), half, 1) for k in (0, 1)
    )
    other = facing(other, 1)
    blocks = [snapshots, along_x(snapshots, 1)]
    behind = along_x(snapshots, X - 1)
    again, late, same, _ = lax.optimization_barrier((snapshots, mass, same, blocks[1]))
    next_first = blocks[1][:, 0] * mass
    folded = jnp.pad(next_first.reshape(-1, half), ((0, PAD - points // half), (0, 0)))
    same = facing(jnp.concatenate([same, folded], axis=0), 0)
    blocks += [along_x(again, 2), behind]
    weighted = call(scale_kernel, (points, width), 1 << 38, again, late[:, None])

    own = call(
        first_kernel, (Y * C, X * r, width), 1 << 30, weighted, *blocks
    )
    own = lax.all_to_all(own, ("y", "c"), 0, 0, tiled=True)
    own = jnp.sum(own, axis=0)
    stack = call(stack_kernel, (X, points, width), 1 << 38, *blocks)
    others = send(stack, lambda z, y, c, x: (z, y, c ^ 1, x))
    after = jnp.pad(jnp.stack([next_first, following * mass]), ((0, PAD - 2), (0, 0)))
    edges = call(edge_kernel, (Y * C, PAD, X * r), 1 << 38, after, *blocks)
    own, stack, others, same, other, edges = lax.optimization_barrier(
        (own, stack, others, same, other, edges)
    )

    far = same[points : points + points // half].reshape(1, points)
    far = jnp.pad(far, ((2, PAD - 3), (0, 0)))
    cross = call(
        second_kernel,
        (Y * C, X * r + PAD, half),
        1 << 30,
        far,
        edges,
        same,
        other,
        stack,
        others,
    )
    cross = lax.all_to_all(cross, ("y", "c"), 0, 0, tiled=True)
    cross = jnp.sum(cross.reshape(Y, C, X * r + PAD, half), axis=0)
    near, end, far = jnp.sum(cross[:, X * r : X * r + 3], axis=0)
    inner = x < X - 1
    edges = jnp.stack(
        [
            jnp.where(inner, near, jnp.where(zh == 0, far, end)),
            jnp.where(inner, far, jnp.where(zh == 0, end, near)),
        ]
    ).reshape(2, X, 1, r)
    edges = jnp.pad(edges, ((0, 0), (0, 0), (0, PAD - 1), (0, half - r)))

    def slots(left, right, edge):
        left, right = left.reshape(X, r, half), right.reshape(X, r, half)
        return turned(jnp.concatenate([left, right, edge], axis=1))

    own = slots(own[:, :half], own[:, half:], edges[0])
    cross = slots(cross[0, : X * r], cross[1, : X * r], edges[1])
    total = lax.all_to_all(sides(own, cross), "zl", 0, 0, tiled=True)
    total = jnp.sum(total, axis=0)
    moved = (zl >= X) == (zh == 0)
    return finish(moved, total, send(total, home))


def solution(mesh):
    fine = Mesh(mesh.devices.reshape(SIZES), NAMES)
    rows, columns = ("zl", "y", "c"), ("zh", "x")
    return jax.shard_map(
        shards,
        mesh=fine,
        in_specs=(P(rows, columns), P(rows), P(rows)),
        out_specs=(P(rows, columns), P(rows, columns)),
        check_vma=False,
    )
```

```python
import jax
import jax.numpy as jnp
import numpy as np
from jax import lax
from jax.experimental import pallas as pl
from jax.experimental.pallas import tpu as pltpu
from jax.sharding import Mesh, PartitionSpec as P

NAMES = ("zl", "y", "c", "zh", "x")
SIZES = (8, 4, 2, 2, 4)
ZL, Y, C, ZH, X = SIZES
FLAT = ZL * Y * C * ZH * X
PAD = 8


def routes(move):
    pairs = []
    for source in range(FLAT):
        zl, y, c, zh, x = (int(v) for v in np.unravel_index(source, SIZES))
        target = move(zh * ZL + zl, y, c, x)
        if target is None:
            continue
        z, y, c, x = target
        z = z % (ZH * ZL)
        place = (z % ZL, y % Y, c % C, z // ZL, x % X)
        pairs.append((source, int(np.ravel_multi_index(place, SIZES))))
    return pairs


def send(value, move):
    return lax.ppermute(value, NAMES, routes(move))


def home(z, y, c, x):
    half = ZL // 2
    if half <= z < ZL:
        return (z + half, y, c, x)
    if ZL <= z < ZL + half:
        return (z - half, y, c, x)
    return None


def call(kernel, out, flops, *operands):
    return pl.pallas_call(
        kernel,
        out_shape=jax.ShapeDtypeStruct(out, jnp.float32),
        in_specs=[pl.BlockSpec(memory_space=pltpu.VMEM)] * len(operands),
        out_specs=pl.BlockSpec(memory_space=pltpu.VMEM),
        compiler_params=pltpu.CompilerParams(vmem_limit_bytes=20 << 20),
        cost_estimate=pl.CostEstimate(
            flops=flops, bytes_accessed=1 << 23, transcendentals=0
        ),
    )(*operands)


def split(value):
    high = value.astype(jnp.bfloat16)
    return high, (value - high.astype(jnp.float32)).astype(jnp.bfloat16)


def prepare(columns):
    high, low = split(columns.T)
    return high, jnp.concatenate([high, low], axis=0)


def product(prepared, rows):
    high, both = prepared
    size = high.shape[0]
    rows_high, rows_low = split(rows)
    part = jnp.dot(both, rows_high, preferred_element_type=jnp.float32)
    rest = jnp.dot(high, rows_low, preferred_element_type=jnp.float32)
    return part[:size] + part[size:] + rest


def scale_kernel(value_ref, weight_ref, out_ref):
    out_ref[...] = value_ref[...] * weight_ref[...]


def stack_kernel(*refs):
    for k, ref in enumerate(refs[:-1]):
        refs[-1][k] = ref[...]


def first_kernel(columns_ref, *refs):
    out_ref = refs[-1]
    width = columns_ref.shape[1]
    r = width // (Y * C)
    prepared = prepare(columns_ref[...])
    for k, ref in enumerate(refs[:-1]):
        value = product(prepared, ref[...]).T
        out_ref[:, k * r : (k + 1) * r, :] = value.reshape(Y * C, r, width)


def rows_of(values, g):
    r = values[0].shape[1] // (Y * C)
    return jnp.concatenate([value[:, g * r : (g + 1) * r] for value in values], axis=1)


def edge_kernel(after_ref, *refs):
    high, low = split(after_ref[...])
    after = (high, jnp.concatenate([high, low], axis=0))
    values = [product(after, ref[...]) for ref in refs[:-1]]
    for g in range(Y * C):
        refs[-1][g] = rows_of(values, g)


def second_kernel(edges_ref, same_ref, other_ref, blocks_ref, others_ref, out_ref):
    count, points, width = blocks_ref.shape
    size = other_ref.shape[1]
    r = width // (Y * C)
    far = jnp.concatenate(
        [same_ref[points + k : points + k + 1] for k in range(points // size)], axis=1
    )
    far = jnp.broadcast_to(far, (PAD, points)).T[:, :1]
    here = prepare(same_ref[:points])
    there = prepare(other_ref[...])
    values = []
    for k in range(count):
        block = blocks_ref[k]
        value = product(here, block) + product(there, others_ref[k])
        out_ref[:, k * r : (k + 1) * r, :] = value.T.reshape(Y * C, r, size)
        values.append(jnp.sum(block * far, axis=0, keepdims=True))
    line = lax.broadcasted_iota(jnp.int32, (PAD, count * r), 0)
    for g in range(Y * C):
        row = jnp.broadcast_to(rows_of(values, g), (PAD, count * r))
        out_ref[g, count * r :, :] = edges_ref[g] + jnp.where(line == 2, row, 0.0)


def finish_kernel(moved_ref, mine_ref, sent_ref, tile_ref, later_ref):
    r, width = tile_ref.shape
    half = width // 2
    value = jnp.where(moved_ref[0] > 0, sent_ref[...], mine_ref[...])
    tile = jnp.concatenate([value[:r], value[r : 2 * r]], axis=1)
    row = lax.broadcasted_iota(jnp.int32, (r, half), 0)
    lane = lax.broadcasted_iota(jnp.int32, (r, half), 1)
    edge = jnp.broadcast_to(value[2 * r : 2 * r + 1], (r, half))
    edge = jnp.sum(jnp.where(row == lane, edge, 0.0), axis=1, keepdims=True)
    lane = lax.broadcasted_iota(jnp.int32, (r, width), 1)
    tile_ref[...] = tile
    later_ref[...] = jnp.where(
        lane == width - 1, edge, pltpu.roll(tile, width - 1, axis=1)
    )


def finish(moved, mine, sent):
    r, width = (mine.shape[0] - PAD) // 2, 2 * mine.shape[1]
    vmem = pl.BlockSpec(memory_space=pltpu.VMEM)
    return pl.pallas_call(
        finish_kernel,
        out_shape=[jax.ShapeDtypeStruct((r, width), jnp.float32)] * 2,
        in_specs=[pl.BlockSpec(memory_space=pltpu.SMEM), vmem, vmem],
        out_specs=[vmem, vmem],
    )(moved.astype(jnp.int32).reshape(1), mine, sent)


def shards(snapshots, following, mass):
    points, width = snapshots.shape
    half, r = width // 2, width // (Y * C)
    x, zh, zl = lax.axis_index("x"), lax.axis_index("zh"), lax.axis_index("zl")
    core = lax.axis_index("c")

    def along_x(value, k):
        return send(value, lambda z, y, c, x: (z, y, c, x - k))

    def facing(value, k):
        return send(value, lambda z, y, c, x: (z + ZL, y, c ^ k, x))

    def turned(value):
        return lax.dynamic_slice_in_dim(
            jnp.concatenate([value, value]), (X - x) & (X - 1), X, 0
        )

    def sides(own, cross):
        return jnp.where(
            zh == 0,
            jnp.concatenate([own, cross]),
            jnp.concatenate([cross, own]),
        )

    columns = snapshots * mass[:, None]
    same, other = (
        lax.dynamic_slice_in_dim(columns, half * (core ^ k), half, 1) for k in (0, 1)
    )
    other = facing(other, 1)
    blocks = [snapshots, along_x(snapshots, 1)]
    behind = along_x(snapshots, X - 1)
    again, late, same, _ = lax.optimization_barrier((snapshots, mass, same, blocks[1]))
    next_first = blocks[1][:, 0] * mass
    folded = jnp.pad(next_first.reshape(-1, half), ((0, PAD - points // half), (0, 0)))
    same = facing(jnp.concatenate([same, folded], axis=0), 0)
    blocks += [along_x(again, 2), behind]
    weighted = call(scale_kernel, (points, width), 1 << 38, again, late[:, None])

    own = call(
        first_kernel, (Y * C, X * r, width), 1 << 30, weighted, *blocks
    )
    own = lax.all_to_all(own, ("y", "c"), 0, 0, tiled=True)
    own = jnp.sum(own, axis=0)
    stack = call(stack_kernel, (X, points, width), 1 << 38, *blocks)
    others = send(stack, lambda z, y, c, x: (z, y, c ^ 1, x))
    after = jnp.pad(jnp.stack([next_first, following * mass]), ((0, PAD - 2), (0, 0)))
    edges = call(edge_kernel, (Y * C, PAD, X * r), 1 << 38, after, *blocks)
    own, stack, others, same, other, edges = lax.optimization_barrier(
        (own, stack, others, same, other, edges)
    )

    cross = call(
        second_kernel,
        (Y * C, X * r + PAD, half),
        1 << 30,
        edges,
        same,
        other,
        stack,
        others,
    )
    cross = lax.all_to_all(cross, ("y", "c"), 0, 0, tiled=True)
    cross = jnp.sum(cross.reshape(Y, C, X * r + PAD, half), axis=0)
    near, end, far = jnp.sum(cross[:, X * r : X * r + 3], axis=0)
    inner = x < X - 1
    edges = jnp.stack(
        [
            jnp.where(inner, near, jnp.where(zh == 0, far, end)),
            jnp.where(inner, far, jnp.where(zh == 0, end, near)),
        ]
    ).reshape(2, X, 1, r)
    edges = jnp.pad(edges, ((0, 0), (0, 0), (0, PAD - 1), (0, half - r)))

    def slots(left, right, edge):
        left, right = left.reshape(X, r, half), right.reshape(X, r, half)
        return turned(jnp.concatenate([left, right, edge], axis=1))

    own = slots(own[:, :half], own[:, half:], edges[0])
    cross = slots(cross[0, : X * r], cross[1, : X * r], edges[1])
    total = lax.all_to_all(sides(own, cross), "zl", 0, 0, tiled=True)
    total = jnp.sum(total, axis=0)
    moved = (zl >= X) == (zh == 0)
    return finish(moved, total, send(total, home))


def solution(mesh):
    fine = Mesh(mesh.devices.reshape(SIZES), NAMES)
    rows, columns = ("zl", "y", "c"), ("zh", "x")
    return jax.shard_map(
        shards,
        mesh=fine,
        in_specs=(P(rows, columns), P(rows), P(rows)),
        out_specs=(P(rows, columns), P(rows, columns)),
        check_vma=False,
    )
```

```python
import jax
import jax.numpy as jnp
import numpy as np
from jax import lax
from jax.experimental import pallas as pl
from jax.experimental.pallas import tpu as pltpu
from jax.sharding import Mesh, PartitionSpec as P

NAMES = ("zl", "y", "c", "zh", "x")
SIZES = (8, 4, 2, 2, 4)
ZL, Y, C, ZH, X = SIZES
FLAT = ZL * Y * C * ZH * X
PAD = 8


def routes(move):
    pairs = []
    for source in range(FLAT):
        zl, y, c, zh, x = (int(v) for v in np.unravel_index(source, SIZES))
        target = move(zh * ZL + zl, y, c, x)
        if target is None:
            continue
        z, y, c, x = target
        z = z % (ZH * ZL)
        place = (z % ZL, y % Y, c % C, z // ZL, x % X)
        pairs.append((source, int(np.ravel_multi_index(place, SIZES))))
    return pairs


def send(value, move):
    return lax.ppermute(value, NAMES, routes(move))


def home(z, y, c, x):
    half = ZL // 2
    if half <= z < ZL:
        return (z + half, y, c, x)
    if ZL <= z < ZL + half:
        return (z - half, y, c, x)
    return None


def call(kernel, out, flops, *operands):
    return pl.pallas_call(
        kernel,
        out_shape=jax.ShapeDtypeStruct(out, jnp.float32),
        in_specs=[pl.BlockSpec(memory_space=pltpu.VMEM)] * len(operands),
        out_specs=pl.BlockSpec(memory_space=pltpu.VMEM),
        compiler_params=pltpu.CompilerParams(vmem_limit_bytes=20 << 20),
        cost_estimate=pl.CostEstimate(
            flops=flops, bytes_accessed=1 << 23, transcendentals=0
        ),
    )(*operands)


def split(value):
    high = value.astype(jnp.bfloat16)
    return high, (value - high.astype(jnp.float32)).astype(jnp.bfloat16)


def prepare(columns):
    high, low = split(columns.T)
    return high, jnp.concatenate([high, low], axis=0)


def product(prepared, rows):
    high, both = prepared
    size = high.shape[0]
    rows_high, rows_low = split(rows)
    part = jnp.dot(both, rows_high, preferred_element_type=jnp.float32)
    rest = jnp.dot(high, rows_low, preferred_element_type=jnp.float32)
    return part[:size] + part[size:] + rest


def scale_kernel(value_ref, weight_ref, out_ref):
    out_ref[...] = value_ref[...] * weight_ref[...]


def stack_kernel(*refs):
    for k, ref in enumerate(refs[:-1]):
        refs[-1][k] = ref[...]


def first_kernel(columns_ref, *refs):
    out_ref = refs[-1]
    width = columns_ref.shape[1]
    r = width // (Y * C)
    prepared = prepare(columns_ref[...])
    for k, ref in enumerate(refs[:-1]):
        value = product(prepared, ref[...]).T
        out_ref[:, k * r : (k + 1) * r, :] = value.reshape(Y * C, r, width)


def rows_of(values, g):
    r = values[0].shape[1] // (Y * C)
    return jnp.concatenate([value[:, g * r : (g + 1) * r] for value in values], axis=1)


def edge_kernel(after_ref, *refs):
    high, low = split(after_ref[...])
    after = (high, jnp.concatenate([high, low], axis=0))
    values = [product(after, ref[...]) for ref in refs[:-1]]
    for g in range(Y * C):
        refs[-1][g] = rows_of(values, g)


def second_kernel(edges_ref, same_ref, other_ref, blocks_ref, others_ref, out_ref):
    count, points, width = blocks_ref.shape
    size = other_ref.shape[1]
    r = width // (Y * C)
    far = jnp.concatenate(
        [same_ref[points + k : points + k + 1] for k in range(points // size)], axis=1
    )
    far = jnp.broadcast_to(far, (PAD, points)).T[:, :1]
    here = prepare(same_ref[:points])
    there = prepare(other_ref[...])
    values = []
    for k in range(count):
        block = blocks_ref[k]
        value = product(here, block) + product(there, others_ref[k])
        out_ref[:, k * r : (k + 1) * r, :] = value.T.reshape(Y * C, r, size)
        values.append(jnp.sum(block * far, axis=0, keepdims=True))
    line = lax.broadcasted_iota(jnp.int32, (PAD, count * r), 0)
    for g in range(Y * C):
        row = jnp.broadcast_to(rows_of(values, g), (PAD, count * r))
        out_ref[g, count * r :, :] = edges_ref[g] + jnp.where(line == 2, row, 0.0)


def finish_kernel(mine_ref, sent_ref, tile_ref, later_ref):
    r, width = tile_ref.shape
    half = width // 2
    moved = (lax.axis_index("zl") >= X) == (lax.axis_index("zh") == 0)
    value = jnp.where(moved, sent_ref[...], mine_ref[...])
    tile = jnp.concatenate([value[:r], value[r : 2 * r]], axis=1)
    row = lax.broadcasted_iota(jnp.int32, (r, half), 0)
    lane = lax.broadcasted_iota(jnp.int32, (r, half), 1)
    edge = jnp.broadcast_to(value[2 * r : 2 * r + 1], (r, half))
    edge = jnp.sum(jnp.where(row == lane, edge, 0.0), axis=1, keepdims=True)
    lane = lax.broadcasted_iota(jnp.int32, (r, width), 1)
    tile_ref[...] = tile
    later_ref[...] = jnp.where(
        lane == width - 1, edge, pltpu.roll(tile, width - 1, axis=1)
    )


def finish(mine, sent):
    r, width = (mine.shape[0] - PAD) // 2, 2 * mine.shape[1]
    vmem = pl.BlockSpec(memory_space=pltpu.VMEM)
    return pl.pallas_call(
        finish_kernel,
        out_shape=[jax.ShapeDtypeStruct((r, width), jnp.float32)] * 2,
        in_specs=[vmem, vmem],
        out_specs=[vmem, vmem],
    )(mine, sent)


def shards(snapshots, following, mass):
    points, width = snapshots.shape
    half, r = width // 2, width // (Y * C)
    x, zh = lax.axis_index("x"), lax.axis_index("zh")
    core = lax.axis_index("c")

    def along_x(value, k):
        return send(value, lambda z, y, c, x: (z, y, c, x - k))

    def facing(value, k):
        return send(value, lambda z, y, c, x: (z + ZL, y, c ^ k, x))

    def turned(value):
        return lax.dynamic_slice_in_dim(
            jnp.concatenate([value, value]), (X - x) & (X - 1), X, 0
        )

    def sides(own, cross):
        return jnp.where(
            zh == 0,
            jnp.concatenate([own, cross]),
            jnp.concatenate([cross, own]),
        )

    columns = snapshots * mass[:, None]
    same, other = (
        lax.dynamic_slice_in_dim(columns, half * (core ^ k), half, 1) for k in (0, 1)
    )
    other = facing(other, 1)
    blocks = [snapshots, along_x(snapshots, 1)]
    behind = along_x(snapshots, X - 1)
    again, late, same, _ = lax.optimization_barrier((snapshots, mass, same, blocks[1]))
    next_first = blocks[1][:, 0] * mass
    folded = jnp.pad(next_first.reshape(-1, half), ((0, PAD - points // half), (0, 0)))
    same = facing(jnp.concatenate([same, folded], axis=0), 0)
    blocks += [along_x(again, 2), behind]
    weighted = call(scale_kernel, (points, width), 1 << 38, again, late[:, None])

    own = call(
        first_kernel, (Y * C, X * r, width), 1 << 30, weighted, *blocks
    )
    own = lax.all_to_all(own, ("y", "c"), 0, 0, tiled=True)
    own = jnp.sum(own, axis=0)
    stack = call(stack_kernel, (X, points, width), 1 << 38, *blocks)
    others = send(stack, lambda z, y, c, x: (z, y, c ^ 1, x))
    after = jnp.pad(jnp.stack([next_first, following * mass]), ((0, PAD - 2), (0, 0)))
    edges = call(edge_kernel, (Y * C, PAD, X * r), 1 << 38, after, *blocks)
    own, stack, others, same, other, edges = lax.optimization_barrier(
        (own, stack, others, same, other, edges)
    )

    cross = call(
        second_kernel,
        (Y * C, X * r + PAD, half),
        1 << 30,
        edges,
        same,
        other,
        stack,
        others,
    )
    cross = lax.all_to_all(cross, ("y", "c"), 0, 0, tiled=True)
    cross = jnp.sum(cross.reshape(Y, C, X * r + PAD, half), axis=0)
    near, end, far = jnp.sum(cross[:, X * r : X * r + 3], axis=0)
    inner = x < X - 1
    edges = jnp.stack(
        [
            jnp.where(inner, near, jnp.where(zh == 0, far, end)),
            jnp.where(inner, far, jnp.where(zh == 0, end, near)),
        ]
    ).reshape(2, X, 1, r)
    edges = jnp.pad(edges, ((0, 0), (0, 0), (0, PAD - 1), (0, half - r)))

    def slots(left, right, edge):
        left, right = left.reshape(X, r, half), right.reshape(X, r, half)
        return turned(jnp.concatenate([left, right, edge], axis=1))

    own = slots(own[:, :half], own[:, half:], edges[0])
    cross = slots(cross[0, : X * r], cross[1, : X * r], edges[1])
    total = lax.all_to_all(sides(own, cross), "zl", 0, 0, tiled=True)
    total = jnp.sum(total, axis=0)
    return finish(total, send(total, home))


def solution(mesh):
    fine = Mesh(mesh.devices.reshape(SIZES), NAMES)
    rows, columns = ("zl", "y", "c"), ("zh", "x")
    return jax.shard_map(
        shards,
        mesh=fine,
        in_specs=(P(rows, columns), P(rows), P(rows)),
        out_specs=(P(rows, columns), P(rows, columns)),
        check_vma=False,
    )
```
